128 devices in a mesh: tm: 32 (over z, x, y_hi), rows: 4 (over y_lo, core).
Axes of the slice: x: 4, y: 4 (y_hi: 2, y_lo: 2; y = y_hi * 2 + y_lo), z: 4, core: 2. Of those that a mesh axis runs over, the one named last changes fastest.
Arguments:
- video: bfloat16 [256, 32, 128, 128], P('tm', 'rows'), may hold values from -36 to 50
- conv_weight: bfloat16 [3, 3, 3, 128, 256], replicated, may hold values from -0.109375 to 0.109375
- norm_gain: float32 [256], replicated, may hold values from 0.5 to 1.5
- norm_bias: float32 [256], replicated, may hold values from -3 to 3
Outputs:
- patch_tokens: bfloat16 [16, 64, 256, 1024], P('rows', 'tm')
The draws below stay inside these ranges and needn't reach their ends.
All inputs are finite; a program needn't handle non-finite values.
Results may differ from the reference program's by a relative error of at most 0.0049.
Values may be sent and summed in bfloat16 or wider, within the bound.
A program may use at most 128 MiB of HBM per device.

```python
import jax
import jax.numpy as jnp
from jax import lax

C_IN = 128
CO = 256
GROUPS = 32
F_DEV = 8
W = 128
FRAMES = 256
NH = 32
N_TM = 32


def draw_video(key, part):
    key_noise = jax.random.fold_in(key, 11)
    key_channel = jax.random.fold_in(key, 12)
    full_shape = (FRAMES, NH, W, C_IN)
    frame_pos = jnp.arange(FRAMES, dtype=jnp.float32) / max(FRAMES - 1, 1)
    channel_scale = jnp.exp(jax.random.uniform(key_channel, (C_IN,), jnp.float32, jnp.log(0.5), jnp.log(2.0)))
    ramp = jnp.exp(frame_pos * jnp.log(3.0))
    noise = jnp.clip(jax.random.normal(key_noise, full_shape, jnp.float32), -6.0, 6.0) + 1.0
    return (noise * ramp[:, None, None, None] * channel_scale).astype(jnp.bfloat16)


def normal_values(rng, dims, scale, bound, kind=jnp.bfloat16):
    array = jax.random.normal(rng, dims, jnp.float32) * scale
    return jnp.minimum(jnp.maximum(array, -bound), bound).astype(kind)


def setup_inputs(seed: int = 0) -> dict:
    streams_of = jax.random.split(jax.random.key(seed), 5)
    return {
        "video": draw_video(jax.random.fold_in(streams_of[4], 71), 0),
        "conv_weight": normal_values(streams_of[1], (3, 3, 3, C_IN, CO), (27 * C_IN) ** -0.5, 0.109375),
        "norm_gain": jnp.clip(1.0 + 0.1 * jax.random.normal(streams_of[2], (CO,), jnp.float32), 0.5, 1.5),
        "norm_bias": normal_values(streams_of[3], (CO,), 0.5, 3.0, jnp.float32),
    }


inv_root = 0.7071067811865476

def reference(video, conv_weight, norm_gain, norm_bias):
    blocks = N_TM
    current = video.astype(jnp.float32).reshape(blocks, F_DEV, -1)
    for level_bit in range(3):
        span = 2 ** level_bit
        arranged = current.reshape(blocks // (2 * span), 2, span, F_DEV, -1)
        first_half = arranged[:, 0]
        second_half = arranged[:, 1]
        current = jnp.stack(((first_half + second_half) * inv_root, (first_half - second_half) * inv_root), 1)
        current = current.reshape(blocks, F_DEV, -1)
    wavelet = current.reshape(FRAMES, NH, W, C_IN).astype(jnp.bfloat16)
    padded = jnp.pad(wavelet.astype(jnp.float32), ((2, 0), (1, 1), (1, 1), (0, 0)))
    convolved = lax.conv_general_dilated(padded[None], conv_weight.astype(jnp.float32), (1, 1, 1), 'VALID', dimension_numbers=('NDHWC', 'DHWIO', 'NDHWC'), precision=lax.Precision.HIGHEST)[0]
    groups = convolved.reshape(FRAMES, NH, W, GROUPS, CO // GROUPS)
    group_mean = lax.optimization_barrier(jnp.mean(groups, axis=(0, 1, 2, 4), keepdims=True))
    centered = groups - group_mean
    variance = lax.optimization_barrier(jnp.mean(centered * centered, axis=(0, 1, 2, 4), keepdims=True))
    normed = (centered / jnp.sqrt(variance + 1e-05)).reshape(FRAMES, NH, W, CO)
    activated = jax.nn.silu(normed * norm_gain + norm_bias).astype(jnp.bfloat16)
    arranged = activated.reshape(FRAMES, NH // 2, 2, W // 2, 2, CO).transpose(1, 3, 0, 2, 4, 5)
    return arranged.reshape(NH // 2, W // 2, FRAMES, 4 * CO)
```

```python
import jax
import jax.numpy as jnp
from jax import lax
from jax.experimental import pallas as pl
from jax.experimental.pallas import tpu as pltpu
from jax.sharding import PartitionSpec as P

MESH = pl.DeviceIdType.MESH
F32 = jnp.float32
BF16 = jnp.bfloat16

NZ, NX, NY, NR = 4, 4, 2, 4
C = 128
CO = 256
HALF_ROOT = 0.35355339059327373
T_ROWS = 272
RANGES = {0: (16, 48), 1: (64, 64), 3: (208, 64), 2: (128, 80)}
PIECES = {0: ((16, 48),), 1: ((64, 64),), 3: ((208, 48), (256, 16)), 2: ((128, 64), (192, 16))}


def exchange_conv(
    video, weight, gain, bias,
    conv_out, norm_out,
    src, zbuf, xbuf, ybuf, edge, halo, wave, taps, acc, w_vmem, st,
    z_s, z_r, x_s, x_r, y_s, y_r, l_s, h_s, h_r, st_s, st_r, w_s, o_s,
):
    me = lax.axis_index("tm")
    r = lax.axis_index("rows")
    z, x, y = me // 8, (me // 2) % 4, me % 2

    def at(z, x, y):
        return {"tm": z * 8 + x * 2 + y}

    weights = pltpu.make_async_copy(weight, w_vmem, w_s)
    weights.start()

    barrier = pltpu.get_barrier_semaphore()
    for d in (1, 2, 3):
        for peer in (at((z + d) % 4, x, y), at(z, (x + d) % 4, y), {"rows": (r + d) % 4}):
            pl.semaphore_signal(barrier, inc=1, device_id=peer, device_id_type=MESH)
    pl.semaphore_signal(barrier, inc=1, device_id=at(z, x, 1 - y), device_id_type=MESH)

    src[0] = jnp.zeros((64, C), BF16)
    src[129] = jnp.zeros((64, C), BF16)

    def turn(pair, carry):
        rows = pl.ds(pl.multiple_of(pair * 16, 16), 16)
        for w0 in range(0, 128, 32):
            two = [jnp.swapaxes(video[:, 2 * pair + k, pl.ds(w0, 32), :], 0, 1) for k in range(2)]
            src[pl.ds(1 + w0, 32), rows, :] = jnp.concatenate(two, axis=1)
        return carry

    lax.fori_loop(0, 4, turn, 0)

    @pl.when(r == 0)
    def _():
        halo[:, 0] = jnp.zeros((4, 6, 64, C), BF16)

    @pl.when(r == 3)
    def _():
        halo[:, 1] = jnp.zeros((4, 6, 64, C), BF16)

    pl.semaphore_wait(barrier, 10)

    def zcopy(s):
        zp = (z - s) % 4
        return pltpu.make_async_remote_copy(
            src_ref=src.at[pl.ds(32 * zp, 34)], dst_ref=zbuf.at[s - 1],
            send_sem=z_s.at[s - 1], recv_sem=z_r.at[s - 1],
            device_id=at(zp, x, y), device_id_type=MESH)

    def zcols(s, first, n):
        return src.at[pl.ds(32 * z + first, n)] if s == 0 else zbuf.at[s - 1, pl.ds(first, n)]

    def xcopy(s, d):
        xp = (x + d) % 4
        return pltpu.make_async_remote_copy(
            src_ref=zcols(s, 8 * xp, 10), dst_ref=xbuf.at[s, x],
            send_sem=x_s.at[s, d], recv_sem=x_r.at[s, d],
            device_id=at(z, xp, y), device_id_type=MESH)

    def xlocal(s):
        return pltpu.make_async_copy(zcols(s, 8 * x, 10), xbuf.at[s, x], l_s.at[s])

    def ycopy(s, d):
        xs = (x - d) % 4
        if isinstance(d, int) and d == 0:
            part = zcols(s, 8 * x + 4 * (1 - y), 6)
        else:
            part = xbuf.at[s, xs, pl.ds(4 * (1 - y), 6)]
        return pltpu.make_async_remote_copy(
            src_ref=part, dst_ref=ybuf.at[s, xs],
            send_sem=y_s.at[s, d], recv_sem=y_r.at[s, d],
            device_id=at(z, x, 1 - y), device_id_type=MESH)

    def begin(s):
        for d in (1, 3, 2):
            xcopy(s, d).start()
        xlocal(s).start()
        ycopy(s, 0).start()

    def forward(s, d):
        xcopy(s, d).wait_recv()
        ycopy(s, d).start()

    def up(s):
        return pltpu.make_async_remote_copy(
            src_ref=edge.at[s, 0], dst_ref=halo.at[s, 1],
            send_sem=h_s.at[s, 0], recv_sem=h_r.at[s, 1],
            device_id={"rows": r - 1}, device_id_type=MESH)

    def down(s):
        return pltpu.make_async_remote_copy(
            src_ref=edge.at[s, 1], dst_ref=halo.at[s, 0],
            send_sem=h_s.at[s, 1], recv_sem=h_r.at[s, 0],
            device_id={"rows": r + 1}, device_id_type=MESH)

    sign = jnp.where(y == 0, HALF_ROOT, -HALF_ROOT).astype(F32)

    def packet(s, w, h0, n):
        rows = pl.ds(h0 * 8, n * 8)
        even, odd = [], []
        for xs in range(4):
            a = xbuf[s, xs, 4 * y + w, rows, :].astype(F32)
            b = ybuf[s, xs, w, rows, :].astype(F32)
            even.append((a + b) * HALF_ROOT)
            odd.append((a - b) * sign)
        out = [None] * 8
        for side, v in ((0, even), (1, odd)):
            p, q, u, t = v[0] + v[1], v[0] - v[1], v[2] + v[3], v[2] - v[3]
            out[0 + side], out[4 + side] = p + u, p - u
            out[2 + side], out[6 + side] = q + t, q - t
        return out

    def waves(s):
        def column(w, carry):
            for h0 in (0, 4):
                blocks = packet(s, w, h0, 4)
                for k in range(4):
                    h = h0 + k
                    line = jnp.concatenate([b[8 * k : 8 * k + 8] for b in blocks], axis=0)
                    wave[w, h + 1, 8 + 64 * s : 72 + 64 * s, :] = line
                    if s == 0:
                        wave[w, h + 1, 264:280, :] = line[:16]
                    if h in (0, 7):
                        edge[s, 0 if h == 0 else 1, w] = line.astype(BF16)
            return carry

        lax.fori_loop(0, 6, column, 0)

        @pl.when(r > 0)
        def _():
            up(s).start()

        @pl.when(r < 3)
        def _():
            down(s).start()

    clip_start = 256 - 64 * z

    def build_taps(s, h_from, h_to):
        r0, n = RANGES[s]
        row = r0 + lax.broadcasted_iota(jnp.int32, (n, C), 0) - clip_start
        outside = [(row >= 0) & (row < 2), row == 0, None]

        def line(i, carry):
            h = h_from + i // 6
            w = i % 6
            for k in range(3):
                v = wave[w, h, 8 + r0 + k - 2 : 8 + r0 + k - 2 + n, :]
                if k < 2:
                    v = jnp.where(outside[k], 0.0, v)
                taps[k, w, h, r0 : r0 + n, :] = v.astype(BF16)
            return carry

        lax.fori_loop(0, 6 * (h_to - h_from), line, 0)

    def take_halo(s):
        @pl.when(r > 0)
        def _():
            down(s).wait_recv()

        @pl.when(r < 3)
        def _():
            up(s).wait_recv()

        def column(w, carry):
            for side, h in ((0, 0), (1, 9)):
                line = halo[s, side, w].astype(F32)
                wave[w, h, 8 + 64 * s : 72 + 64 * s, :] = line
                if s == 0:
                    wave[w, h, 264:280, :] = line[:16]
            return carry

        lax.fori_loop(0, 6, column, 0)

    count = [0]
    st[0] = jnp.zeros((8, CO), F32)

    def add_stats(out, m):
        mean = jnp.sum(out, axis=0, keepdims=True) * (1.0 / m)
        d = out - mean
        return mean, jnp.sum(d * d, axis=0, keepdims=True)

    def merge(a, b):
        (na, ma, qa), (nb, mb, qb) = a, b
        n = na + nb
        delta = mb - ma
        return n, ma + delta * (nb / n), qa + qb + delta * delta * (na * nb / n)

    def conv_pairs(s, hooks):
        r0, n = RANGES[s]

        def chunk(m, carry):
            h = 1 + 2 * m
            parts = []
            for k in range(3):
                for i in range(3):
                    for j in range(3):
                        v = taps[k, j : j + 4, pl.ds(h + i, 2), r0 : r0 + n, :]
                        parts.append(v.reshape(8 * n, C))
            out = jnp.dot(jnp.concatenate(parts, axis=1), w_vmem[...], preferred_element_type=F32)
            for w in range(4):
                for a in range(2):
                    piece = out[(2 * w + a) * n : (2 * w + a + 1) * n]
                    lane = ((1 - a) * 2 + w % 2) * CO
                    acc[m + a, w // 2, r0 : r0 + n, lane : lane + CO] = piece
            mean, sq = add_stats(out, 8 * n)
            st[1, pl.ds(m, 1), :] = mean
            st[2, pl.ds(m, 1), :] = sq
            if hooks is not None:
                hooks(m)
            return carry

        lax.fori_loop(0, 3, chunk, 0)

    def conv_edges(s):
        r0, n = RANGES[s]
        parts = []
        for k in range(3):
            for i in range(3):
                for j in range(3):
                    top = taps[k, j : j + 4, i, r0 : r0 + n, :].reshape(4 * n, C)
                    low = taps[k, j : j + 4, 7 + i, r0 : r0 + n, :].reshape(4 * n, C)
                    parts.append(jnp.concatenate([top, low], axis=0))
        out = jnp.dot(jnp.concatenate(parts, axis=1), w_vmem[...], preferred_element_type=F32)
        for w in range(4):
            for a, p in ((0, 0), (1, 3)):
                piece = out[(4 * a + w) * n : (4 * a + w + 1) * n]
                lane = (a * 2 + w % 2) * CO
                acc[p, w // 2, r0 : r0 + n, lane : lane + CO] = piece
        mean, sq = add_stats(out, 8 * n)
        st[1, 3:4, :] = mean
        st[2, 3:4, :] = sq

    def out_copies(s):
        copies = []
        for i, (first, n) in enumerate(PIECES[s]):
            t = (64 * z + first) % 256
            copies.append(
                pltpu.make_async_copy(
                    acc.at[:, :, pl.ds(first, n), :],
                    conv_out.at[:, :, pl.ds(pl.multiple_of(t, 16), n), :],
                    o_s.at[s, i]))
        return copies

    def finish(s):
        n = 8 * RANGES[s][1]
        total = None
        for m in range(4):
            term = (n, st[1, m : m + 1, :], st[2, m : m + 1, :])
            total = term if total is None else merge(total, term)
        if count[0]:
            total = merge((count[0], st[0, 0:1, :], st[0, 1:2, :]), total)
        st[0, 0:1, :] = total[1]
        st[0, 1:2, :] = total[2]
        count[0] = total[0]
        for copy in out_copies(s):
            copy.start()

    def arrive(s):
        xlocal(s).wait()
        for d in range(4):
            ycopy(s, d).wait_recv()

    def hook(s):
        def run(m):
            forward(s, 1 + 2 * m - 3 * (m // 2))
        return run

    def stage(s, hooks):
        arrive(s)
        waves(s)
        build_taps(s, 1, 9)
        conv_pairs(s, hooks)
        take_halo(s)
        build_taps(s, 0, 1)
        build_taps(s, 9, 10)
        conv_edges(s)
        finish(s)

    zcopy(1).start()
    zcopy(3).start()
    begin(0)
    for d in (1, 3, 2):
        forward(0, d)
    zcopy(1).wait_recv()
    begin(1)
    zcopy(3).wait_recv()
    zcopy(1).wait_send()
    zcopy(3).wait_send()
    zcopy(2).start()
    begin(3)
    weights.wait()
    stage(0, hook(1))
    stage(1, hook(3))
    zcopy(2).wait_recv()
    begin(2)
    stage(3, hook(2))
    stage(2, None)

    mean, sq = st[0, 0:1, :], st[0, 1:2, :]
    held = float(count[0])
    axes = (
        (NR, r, lambda d: {"rows": (r + d) % 4}, lambda d: (r + d) % 4),
        (NY, y, lambda d: at(z, x, (y + d) % 2), lambda d: (y + d) % 2),
        (NX, x, lambda d: at(z, (x + d) % 4, y), lambda d: (x + d) % 4),
        (NZ, z, lambda d: at((z + d) % 4, x, y), lambda d: (z + d) % 4),
    )
    for level, (size, mine, peer, _) in enumerate(axes):
        base = 3 + 4 * level
        st[base + mine, 0:1, :] = mean
        st[base + mine, 1:2, :] = sq

        def share(d):
            return pltpu.make_async_remote_copy(
                src_ref=st.at[base + mine], dst_ref=st.at[base + mine],
                send_sem=st_s.at[level, d], recv_sem=st_r.at[level, d],
                device_id=peer(d), device_id_type=MESH)

        for d in range(1, size):
            share(d).start()
        for d in range(1, size):
            share(d).wait_recv()
        means = [st[base + i, 0:1, :] for i in range(size)]
        mean = sum(means) * (1.0 / size)
        sq = sum(st[base + i, 1:2, :] for i in range(size))
        sq = sq + held * sum((m - mean) * (m - mean) for m in means)
        held = held * size
        for d in range(1, size):
            share(d).wait_send()

    lane = lax.broadcasted_iota(jnp.int32, (1, CO), 1)

    def over_group(v):
        for bit in (1, 2, 4):
            v = v + jnp.where(lane & bit == 0, pltpu.roll(v, CO - bit, 1), pltpu.roll(v, bit, 1))
        return v

    group_mean = over_group(mean) * (1.0 / 8)
    d = mean - group_mean
    variance = over_group(sq + held * d * d) * (1.0 / (8 * held))
    scale = gain[...] / jnp.sqrt(variance + 1e-05)
    for row, v in enumerate((group_mean, scale, bias[...])):
        norm_out[row : row + 1, :] = jnp.concatenate([v] * 4, axis=1)

    for s in range(4):
        for copy in out_copies(s):
            copy.wait()
        for d in range(4):
            ycopy(s, d).wait_send()
        for d in (1, 2, 3):
            xcopy(s, d).wait_send()

        @pl.when(r > 0)
        def _():
            up(s).wait_send()

        @pl.when(r < 3)
        def _():
            down(s).wait_send()
    zcopy(2).wait_send()


def norm_silu(conv, norm, out):
    half = (conv[...] - norm[0:1, :]) * (0.5 * norm[1:2, :]) + 0.5 * norm[2:3, :]
    out[...] = (half + half * jnp.tanh(half)).astype(BF16)


def per_device(video, conv_weight, norm_gain, norm_bias):
    vmem = pl.BlockSpec(memory_space=pltpu.VMEM)
    anywhere = pl.BlockSpec(memory_space=pl.ANY)
    dma = pltpu.SemaphoreType.DMA
    conv, norm = pl.pallas_call(
        exchange_conv,
        out_shape=(
            jax.ShapeDtypeStruct((4, 2, 256, 1024), F32),
            jax.ShapeDtypeStruct((8, 1024), F32),
        ),
        in_specs=[vmem, anywhere, vmem, vmem],
        out_specs=(anywhere, vmem),
        scratch_shapes=[
            pltpu.VMEM((130, 64, C), BF16),
            pltpu.VMEM((3, 34, 64, C), BF16),
            pltpu.VMEM((4, 4, 10, 64, C), BF16),
            pltpu.VMEM((4, 4, 6, 64, C), BF16),
            pltpu.VMEM((4, 2, 6, 64, C), BF16),
            pltpu.VMEM((4, 2, 6, 64, C), BF16),
            pltpu.VMEM((6, 10, 8 + T_ROWS, C), F32),
            pltpu.VMEM((3, 6, 10, T_ROWS, C), BF16),
            pltpu.VMEM((4, 2, T_ROWS, 1024), F32),
            pltpu.VMEM((27 * C, CO), BF16),
            pltpu.VMEM((19, 8, CO), F32),
            dma((3,)), dma((3,)),
            dma((4, 4)), dma((4, 4)),
            dma((4, 4)), dma((4, 4)),
            dma((4,)),
            dma((4, 2)), dma((4, 2)),
            dma((4, 4)), dma((4, 4)),
            dma, dma((4, 2)),
        ],
        compiler_params=pltpu.CompilerParams(
            collective_id=0, has_side_effects=True, vmem_limit_bytes=60 << 20
        ),
        cost_estimate=pl.CostEstimate(
            flops=2 * 8192 * 3456 * 256, bytes_accessed=16 << 20, transcendentals=0
        ),
    )(video, conv_weight.reshape(27 * C, CO), norm_gain.reshape(1, CO), norm_bias.reshape(1, CO))
    return pl.pallas_call(
        norm_silu,
        out_shape=jax.ShapeDtypeStruct((4, 2, 256, 1024), BF16),
        grid=(4, 2),
        in_specs=[
            pl.BlockSpec((1, 1, 256, 1024), lambda p, q: (p, q, 0, 0)),
            pl.BlockSpec((8, 1024), lambda p, q: (0, 0)),
        ],
        out_specs=pl.BlockSpec((1, 1, 256, 1024), lambda p, q: (p, q, 0, 0)),
        compiler_params=pltpu.CompilerParams(vmem_limit_bytes=16 << 20),
        cost_estimate=pl.CostEstimate(
            flops=2097152 * 6, bytes_accessed=12 << 20, transcendentals=2097152
        ),
    )(conv, norm)


def solution(mesh):
    placed = (P("tm", "rows", None, None), P(), P(), P())
    return jax.shard_map(
        per_device,
        mesh=mesh,
        in_specs=placed,
        out_specs=P("rows", "tm", None, None),
        check_vma=False,
    )
```

```python
import jax
import jax.numpy as jnp
from jax import lax
from jax.experimental import pallas as pl
from jax.experimental.pallas import tpu as pltpu
from jax.sharding import PartitionSpec as P

MESH = pl.DeviceIdType.MESH
F32 = jnp.float32
BF16 = jnp.bfloat16

C = 128
CO = 256
HALF_ROOT = 0.35355339059327373
T_ROWS = 272
RANGES = {0: (16, 48), 1: (64, 64), 3: (208, 64), 2: (128, 80)}
ORDER = [(0, 1), (0, 3), (0, 2)] + [(s, d) for s in (1, 3, 2) for d in (0, 1, 3, 2)]
PIECES = {0: ((16, 48),), 1: ((64, 64),), 3: ((208, 48), (256, 16)), 2: ((128, 64), (192, 16))}


def exchange_conv(
    video_in, weight, gain, bias,
    conv_out, scale_out, shift_out,
    video, src, xbuf, ybuf, edge, halo, wave, taps, acc, w_vmem, st, sums, ref_mean,
    x_s, x_r, y_s, y_r, l_s, h_s, h_r, st_s, st_r, v_s, w_s, o_s,
):
    me = lax.axis_index("tm")
    r = lax.axis_index("rows")
    z, x, y = me // 8, (me // 2) % 4, me % 2

    def at(z, x, y):
        return {"tm": z * 8 + x * 2 + y}

    frames = pltpu.make_async_copy(video_in, video, v_s)
    frames.start()
    barrier = pltpu.get_barrier_semaphore()
    line_of = lambda i: {"tm": z * 8 + x * 2 + ((y + i // 4) & 1), "rows": (r + i) & 3}
    plane_of = lambda i: at((z + i // 4) & 3, (x + i) & 3, y)
    for peer in [line_of(i) for i in range(1, 8)] + [plane_of(i) for i in range(1, 16)]:
        pl.semaphore_signal(barrier, inc=1, device_id=peer, device_id_type=MESH)

    weights = pltpu.make_async_copy(weight, w_vmem, w_s)
    weights.start()

    src[0] = jnp.zeros((64, C), BF16)
    src[129] = jnp.zeros((64, C), BF16)

    def turn(pair, carry):
        rows = pl.ds(pl.multiple_of(pair * 16, 16), 16)
        for w0 in range(0, 128, 32):
            two = [jnp.swapaxes(video[:, 2 * pair + k, pl.ds(w0, 32), :], 0, 1) for k in range(2)]
            src[pl.ds(1 + w0, 32), rows, :] = jnp.concatenate(two, axis=1)
        return carry

    frames.wait()
    lax.fori_loop(0, 4, turn, 0)

    @pl.when(r == 0)
    def _():
        halo[:, 0] = jnp.zeros((4, 6, 64, C), BF16)

    @pl.when(r == 3)
    def _():
        halo[:, 1] = jnp.zeros((4, 6, 64, C), BF16)

    pl.semaphore_wait(barrier, 22)

    def plane(s, d):
        zp, xp = (z - s) & 3, (x + d) & 3
        return pltpu.make_async_remote_copy(
            src_ref=src.at[pl.ds(32 * zp + 8 * xp, 10)], dst_ref=xbuf.at[s, x],
            send_sem=x_s.at[s, d], recv_sem=x_r.at[s, d],
            device_id=at(zp, xp, y), device_id_type=MESH)

    own = pltpu.make_async_copy(src.at[pl.ds(32 * z + 8 * x, 10)], xbuf.at[0, x], l_s)

    def across(s, d, first=False, c0=0, n=6, row=None):
        xs = (x - d) & 3
        if first:
            part = src.at[pl.ds(32 * z + 8 * x + 4 * (1 - y), 6)]
        else:
            part = xbuf.at[s, xs, pl.ds(4 * (1 - y) + c0, n)]
        row = s if row is None else row
        return pltpu.make_async_remote_copy(
            src_ref=part, dst_ref=ybuf.at[s, xs, pl.ds(c0, n)],
            send_sem=y_s.at[row, d], recv_sem=y_r.at[row, d],
            device_id=at(z, x, 1 - y), device_id_type=MESH)

    def last_a(d):
        return across(2, d, False, 0, 4, 2)

    def last_b(d):
        return across(2, d, False, 4, 2, 4)

    def forward(s, d):
        plane(s, d).wait_recv()
        (last_a(d) if s == 2 else across(s, d)).start()

    def up(s, c0, n, row):
        return pltpu.make_async_remote_copy(
            src_ref=edge.at[s, 0, pl.ds(c0, n)], dst_ref=halo.at[s, 1, pl.ds(c0, n)],
            send_sem=h_s.at[row, 0], recv_sem=h_r.at[row, 1],
            device_id={"rows": r - 1}, device_id_type=MESH)

    def down(s, c0, n, row):
        return pltpu.make_async_remote_copy(
            src_ref=edge.at[s, 1, pl.ds(c0, n)], dst_ref=halo.at[s, 0, pl.ds(c0, n)],
            send_sem=h_s.at[row, 1], recv_sem=h_r.at[row, 0],
            device_id={"rows": r + 1}, device_id_type=MESH)

    sign = jnp.where(y == 0, HALF_ROOT, -HALF_ROOT).astype(F32)

    def packet(s, w, h0, n):
        rows = pl.ds(h0 * 8, n * 8)
        even, odd = [], []
        for xs in range(4):
            a = xbuf[s, xs, 4 * y + w, rows, :].astype(F32)
            b = ybuf[s, xs, w, rows, :].astype(F32)
            even.append((a + b) * HALF_ROOT)
            odd.append((a - b) * sign)
        out = [None] * 8
        for side, v in ((0, even), (1, odd)):
            p, q, u, t = v[0] + v[1], v[0] - v[1], v[2] + v[3], v[2] - v[3]
            out[0 + side], out[4 + side] = p + u, p - u
            out[2 + side], out[6 + side] = q + t, q - t
        return out

    def waves(s, c0, n, row):
        def column(w, carry):
            for h0 in (0, 4):
                blocks = packet(s, w, h0, 4)
                for k in range(4):
                    h = h0 + k
                    line = jnp.concatenate([b[8 * k : 8 * k + 8] for b in blocks], axis=0)
                    wave[w, h + 1, 8 + 64 * s : 72 + 64 * s, :] = line
                    if s == 0:
                        wave[w, h + 1, 264:280, :] = line[:16]
                    if h in (0, 7):
                        edge[s, 0 if h == 0 else 1, w] = line.astype(BF16)
            return carry

        lax.fori_loop(c0, c0 + n, column, 0)

        @pl.when(r > 0)
        def _():
            up(s, c0, n, row).start()

        @pl.when(r < 3)
        def _():
            down(s, c0, n, row).start()

    clip_start = 256 - 64 * z

    def build_taps(s, c0, cn, h_from, h_to):
        r0, n = RANGES[s]
        row = r0 + lax.broadcasted_iota(jnp.int32, (n, C), 0) - clip_start
        outside = [(row >= 0) & (row < 2), row == 0, None]

        def line(h, carry):
            for w in range(c0, c0 + cn):
                for k in range(3):
                    v = wave[w, h, 8 + r0 + k - 2 : 8 + r0 + k - 2 + n, :]
                    if k < 2:
                        v = jnp.where(outside[k], 0.0, v)
                    taps[k, w, h, r0 : r0 + n, :] = v.astype(BF16)
            return carry

        lax.fori_loop(h_from, h_to, line, 0)

    def take_halo(s, c0, n, row):
        @pl.when(r > 0)
        def _():
            down(s, c0, n, row).wait_recv()

        @pl.when(r < 3)
        def _():
            up(s, c0, n, row).wait_recv()

        def column(w, carry):
            for side, h in ((0, 0), (1, 9)):
                line = halo[s, side, w].astype(F32)
                wave[w, h, 8 + 64 * s : 72 + 64 * s, :] = line
                if s == 0:
                    wave[w, h, 264:280, :] = line[:16]
            return carry

        lax.fori_loop(c0, c0 + n, column, 0)

    noted = []

    def merge(a, b):
        (na, ma, qa), (nb, mb, qb) = a, b
        n = na + nb
        delta = mb - ma
        return n, ma + delta * (nb / n), qa + qb + delta * delta * (na * nb / n)

    def conv(s, w0, nw, rows, slot, first=None):
        r0, n = RANGES[s]
        parts = []
        for k in range(3):
            for i in range(3):
                for j in range(3):
                    group = [
                        taps[k, w0 + j : w0 + j + nw, pl.ds(h + i, c), r0 : r0 + n, :].reshape(nw * c * n, C)
                        for h, c in rows
                    ]
                    parts.append(group[0] if len(group) == 1 else jnp.concatenate(group, axis=0))
        out = jnp.dot(jnp.concatenate(parts, axis=1), w_vmem[...], preferred_element_type=F32)
        m = out.shape[0]
        mean = jnp.sum(out, axis=0, keepdims=True) * (1.0 / m)
        d = out - mean
        st[1, pl.ds(slot, 1), :] = mean
        st[2, pl.ds(slot, 1), :] = jnp.sum(d * d, axis=0, keepdims=True)
        if first is not None:
            @pl.when(first)
            def _():
                ref_mean[...] = mean

        kept = (out - ref_mean[...]).astype(BF16)
        pieces, base = [], 0
        for h, c in rows:
            pieces.append(kept[base : base + nw * c * n].reshape(nw, c, n, CO))
            base += nw * c * n
        return pieces

    def conv_pairs(s, hooks):
        r0, n = RANGES[s]

        def chunk(m, carry):
            [piece] = conv(s, 0, 4, [(1 + 2 * m, 2)], m, m == 0 if s == 0 else None)
            for w in range(4):
                for a in range(2):
                    lane = ((1 - a) * 2 + w % 2) * CO
                    acc[m + a, w // 2, r0 : r0 + n, lane : lane + CO] = piece[w, a]
            if hooks is not None:
                hooks(m)
            return carry

        lax.fori_loop(0, 3, chunk, 0)
        noted.extend((8 * n, m) for m in range(3))

    def conv_all(s, w0, nw, rows, slot):
        r0, n = RANGES[s]
        pieces = conv(s, w0, nw, rows, slot)
        for (h, c), piece in zip(rows, pieces):
            for w in range(nw):
                for a in range(c):
                    lane = ((h + a) % 2 * 2 + (w0 + w) % 2) * CO
                    acc[(h + a) // 2, (w0 + w) // 2, r0 : r0 + n, lane : lane + CO] = piece[w, a]
        noted.append((nw * sum(c for _, c in rows) * n, slot))

    EDGES = [(0, 1), (7, 1)]

    def out_copies(s):
        copies = []
        for i, (first, n) in enumerate(PIECES[s]):
            t = (64 * z + first) % 256
            copies.append(
                pltpu.make_async_copy(
                    acc.at[:, :, pl.ds(first, n), :],
                    conv_out.at[:, :, pl.ds(pl.multiple_of(t, 16), n), :],
                    o_s.at[s, i]))
        return copies

    def finish(s):
        total = None if s == 0 else (done[0], st[0, 0:1, :], st[0, 1:2, :])
        for n, slot in noted:
            term = (n, st[1, slot : slot + 1, :], st[2, slot : slot + 1, :])
            total = term if total is None else merge(total, term)
        noted.clear()
        st[0, 0:1, :] = total[1]
        st[0, 1:2, :] = total[2]
        done[0] = total[0]
        for copy in out_copies(s):
            copy.start()

    done = [0]

    def arrive(s):
        if s == 0:
            own.wait()
        for d in range(4):
            across(s, d).wait_recv()

    def hook(*three):
        def run(m):
            for i, (s, d) in enumerate(three):
                @pl.when(m == i)
                def _(s=s, d=d):
                    forward(s, d)

        return run

    def stage(s, hooks):
        arrive(s)
        waves(s, 0, 6, s)
        build_taps(s, 0, 6, 1, 9)
        conv_pairs(s, hooks)
        take_halo(s, 0, 6, s)
        build_taps(s, 0, 6, 0, 1)
        build_taps(s, 0, 6, 9, 10)
        conv_all(s, 0, 4, EDGES, 3)
        finish(s)

    def last_whole(s):
        for d in range(4):
            last_a(d).wait_recv()
            last_b(d).wait_recv()
        waves(s, 0, 6, s)
        build_taps(s, 0, 6, 1, 9)
        conv_pairs(s, None)
        take_halo(s, 0, 6, s)
        build_taps(s, 0, 6, 0, 1)
        build_taps(s, 0, 6, 9, 10)
        conv_all(s, 0, 4, EDGES, 3)
        finish(s)

    for s, d in ORDER:
        plane(s, d).start()
    own.start()
    across(0, 0, True).start()
    for d in (1, 3, 2):
        forward(0, d)
    forward(1, 0)
    weights.wait()
    stage(0, hook((1, 1), (1, 3), (1, 2)))
    for d in (0, 1, 3):
        forward(3, d)
    stage(1, hook((3, 2), (2, 0), (2, 1)))
    for d in (3, 2):
        forward(2, d)
    for d in range(4):
        last_b(d).start()
    stage(3, None)
    last_whole(2)

    mean, sq = st[0, 0:1, :], st[0, 1:2, :]
    held = float(done[0])
    axes = (
        (8, 4 * y + r, line_of, lambda i: 4 * ((y + i // 4) & 1) + ((r + i) & 3)),
        (16, 4 * z + x, plane_of, lambda i: 4 * ((z + i // 4) & 3) + ((x + i) & 3)),
    )
    base, shares = 0, []
    for level, (size, mine, peer, slot) in enumerate(axes):
        sums[base + mine, :, :CO] = mean
        sums[base + mine, :, CO:] = sq
        here = [
            pltpu.make_async_remote_copy(
                src_ref=sums.at[base + mine], dst_ref=sums.at[base + mine],
                send_sem=st_s.at[level, i], recv_sem=st_r.at[level, i],
                device_id=peer(i), device_id_type=MESH)
            for i in range(1, size)
        ]
        for share in here:
            share.start()
        for share in here:
            share.wait_recv()
        shares += here
        means = [sums[base + i, :, :CO] for i in range(size)]
        mean = sum(means) * (1.0 / size)
        sq = sum(sums[base + i, :, CO:] for i in range(size))
        sq = sq + held * sum((m - mean) * (m - mean) for m in means)
        held = held * size
        base += size

    lane = lax.broadcasted_iota(jnp.int32, (1, CO), 1)

    def over_group(v):
        for bit in (1, 2, 4):
            v = v + jnp.where(lane & bit == 0, pltpu.roll(v, CO - bit, 1), pltpu.roll(v, bit, 1))
        return v

    group_mean = over_group(mean) * (1.0 / 8)
    d = mean - group_mean
    variance = over_group(sq + held * d * d) * (1.0 / (8 * held))
    scale = 0.5 * gain[...] / jnp.sqrt(variance + 1e-05)
    shift = (ref_mean[...] - group_mean) * scale + 0.5 * bias[...]
    scale_out[...] = jnp.concatenate([scale] * 4, axis=1)
    shift_out[...] = jnp.concatenate([shift] * 4, axis=1)

    for share in shares:
        share.wait_send()
    for d in range(4):
        last_a(d).wait_send()
        last_b(d).wait_send()
    for s in range(4):
        for copy in out_copies(s):
            copy.wait()
        for d in range(4):
            if s != 2:
                across(s, d).wait_send()
            if s or d:
                plane(s, d).wait_send()
        for c0, n, row in ((0, 6, s),):

            @pl.when(r > 0)
            def _():
                up(s, c0, n, row).wait_send()

            @pl.when(r < 3)
            def _():
                down(s, c0, n, row).wait_send()


def per_device(video, conv_weight, norm_gain, norm_bias):
    vmem = pl.BlockSpec(memory_space=pltpu.VMEM)
    anywhere = pl.BlockSpec(memory_space=pl.ANY)
    dma = pltpu.SemaphoreType.DMA
    conv, scale, shift = pl.pallas_call(
        exchange_conv,
        out_shape=(
            jax.ShapeDtypeStruct((4, 2, 256, 1024), BF16),
            jax.ShapeDtypeStruct((1, 1024), F32),
            jax.ShapeDtypeStruct((1, 1024), F32),
        ),
        in_specs=[anywhere, anywhere, vmem, vmem],
        out_specs=(anywhere, vmem, vmem),
        scratch_shapes=[
            pltpu.VMEM((8, 8, 128, C), BF16),
            pltpu.VMEM((130, 64, C), BF16),
            pltpu.VMEM((4, 4, 10, 64, C), BF16),
            pltpu.VMEM((4, 4, 6, 64, C), BF16),
            pltpu.VMEM((4, 2, 6, 64, C), BF16),
            pltpu.VMEM((4, 2, 6, 64, C), BF16),
            pltpu.VMEM((6, 10, 8 + T_ROWS, C), F32),
            pltpu.VMEM((3, 6, 10, T_ROWS, C), BF16),
            pltpu.VMEM((4, 2, T_ROWS, 1024), BF16),
            pltpu.VMEM((27 * C, CO), BF16),
            pltpu.VMEM((3, 8, CO), F32),
            pltpu.VMEM((24, 1, 2 * CO), F32),
            pltpu.VMEM((1, CO), F32),
            dma((4, 4)), dma((4, 4)),
            dma((5, 4)), dma((5, 4)),
            dma,
            dma((5, 2)), dma((5, 2)),
            dma((2, 16)), dma((2, 16)),
            dma, dma, dma((4, 2)),
        ],
        compiler_params=pltpu.CompilerParams(
            collective_id=0, has_side_effects=True, vmem_limit_bytes=60 << 20
        ),
        cost_estimate=pl.CostEstimate(
            flops=2 * 8192 * 3456 * 256, bytes_accessed=16 << 20, transcendentals=0
        ),
    )(video, conv_weight.reshape(27 * C, CO), norm_gain.reshape(1, CO), norm_bias.reshape(1, CO))
    half = conv.astype(F32) * scale[0] + shift[0]
    return (half + half * jnp.tanh(half)).astype(BF16)


def solution(mesh):
    placed = (P("tm", "rows", None, None), P(), P(), P())
    return jax.shard_map(
        per_device,
        mesh=mesh,
        in_specs=placed,
        out_specs=P("rows", "tm", None, None),
        check_vma=False,
    )
```

```python
import jax
import jax.numpy as jnp
from jax import lax
from jax.experimental import pallas as pl
from jax.experimental.pallas import tpu as pltpu
from jax.sharding import PartitionSpec as P

MESH = pl.DeviceIdType.MESH
F32 = jnp.float32
BF16 = jnp.bfloat16

C = 128
CO = 256
HALF_ROOT = 0.35355339059327373
T_ROWS = 272
RANGES = {0: (16, 48), 1: (64, 64), 3: (208, 64), 2: (128, 80)}
ORDER = [(0, 1), (0, 3), (0, 2)] + [(s, d) for s in (1, 3, 2) for d in (0, 1, 3, 2)]
PIECES = {0: ((16, 48),), 1: ((64, 64),), 3: ((208, 48), (256, 16)), 2: ((128, 64), (192, 16))}


def exchange_conv(
    video_in, weight, gain, bias,
    conv_out, scale_out, shift_out,
    video, src, xbuf, ybuf, edge, halo, wave, taps, acc, w_vmem, st, sums, ref_mean,
    x_s, x_r, y_s, y_r, l_s, h_s, h_r, st_s, st_r, v_s, w_s, o_s,
):
    me = lax.axis_index("tm")
    r = lax.axis_index("rows")
    z, x, y = me // 8, (me // 2) % 4, me % 2

    def at(z, x, y):
        return {"tm": z * 8 + x * 2 + y}

    frames = pltpu.make_async_copy(video_in, video, v_s)
    frames.start()
    barrier = pltpu.get_barrier_semaphore()
    line_of = lambda i: {"tm": z * 8 + x * 2 + ((y + i // 4) & 1), "rows": (r + i) & 3}
    plane_of = lambda i: at((z + i // 4) & 3, (x + i) & 3, y)
    for peer in [line_of(i) for i in range(1, 8)] + [plane_of(i) for i in range(1, 16)]:
        pl.semaphore_signal(barrier, inc=1, device_id=peer, device_id_type=MESH)

    weights = pltpu.make_async_copy(weight, w_vmem, w_s)
    weights.start()

    src[0] = jnp.zeros((64, C), BF16)
    src[129] = jnp.zeros((64, C), BF16)

    def turn(pair, carry):
        rows = pl.ds(pl.multiple_of(pair * 16, 16), 16)
        for w0 in range(0, 128, 32):
            two = [jnp.swapaxes(video[:, 2 * pair + k, pl.ds(w0, 32), :], 0, 1) for k in range(2)]
            src[pl.ds(1 + w0, 32), rows, :] = jnp.concatenate(two, axis=1)
        return carry

    frames.wait()
    lax.fori_loop(0, 4, turn, 0)

    @pl.when(r == 0)
    def _():
        halo[:, 0] = jnp.zeros((4, 6, 64, C), BF16)

    @pl.when(r == 3)
    def _():
        halo[:, 1] = jnp.zeros((4, 6, 64, C), BF16)

    pl.semaphore_wait(barrier, 22)

    def plane(s, d):
        zp, xp = (z - s) & 3, (x + d) & 3
        return pltpu.make_async_remote_copy(
            src_ref=src.at[pl.ds(32 * zp + 8 * xp, 10)], dst_ref=xbuf.at[s, x],
            send_sem=x_s.at[s, d], recv_sem=x_r.at[s, d],
            device_id=at(zp, xp, y), device_id_type=MESH)

    own = pltpu.make_async_copy(src.at[pl.ds(32 * z + 8 * x, 10)], xbuf.at[0, x], l_s)

    def across(s, d, first=False, c0=0, n=6, row=None):
        xs = (x - d) & 3
        if first:
            part = src.at[pl.ds(32 * z + 8 * x + 4 * (1 - y), 6)]
        else:
            part = xbuf.at[s, xs, pl.ds(4 * (1 - y) + c0, n)]
        row = s if row is None else row
        return pltpu.make_async_remote_copy(
            src_ref=part, dst_ref=ybuf.at[s, xs, pl.ds(c0, n)],
            send_sem=y_s.at[row, d], recv_sem=y_r.at[row, d],
            device_id=at(z, x, 1 - y), device_id_type=MESH)

    def forward(s, d):
        plane(s, d).wait_recv()
        across(s, d).start()

    def up(s, c0, n, row):
        return pltpu.make_async_remote_copy(
            src_ref=edge.at[s, 0, pl.ds(c0, n)], dst_ref=halo.at[s, 1, pl.ds(c0, n)],
            send_sem=h_s.at[row, 0], recv_sem=h_r.at[row, 1],
            device_id={"rows": r - 1}, device_id_type=MESH)

    def down(s, c0, n, row):
        return pltpu.make_async_remote_copy(
            src_ref=edge.at[s, 1, pl.ds(c0, n)], dst_ref=halo.at[s, 0, pl.ds(c0, n)],
            send_sem=h_s.at[row, 1], recv_sem=h_r.at[row, 0],
            device_id={"rows": r + 1}, device_id_type=MESH)

    sign = jnp.where(y == 0, HALF_ROOT, -HALF_ROOT).astype(F32)

    def packet(s, w, h0, n):
        rows = pl.ds(h0 * 8, n * 8)
        even, odd = [], []
        for xs in range(4):
            a = xbuf[s, xs, 4 * y + w, rows, :].astype(F32)
            b = ybuf[s, xs, w, rows, :].astype(F32)
            even.append((a + b) * HALF_ROOT)
            odd.append((a - b) * sign)
        out = [None] * 8
        for side, v in ((0, even), (1, odd)):
            p, q, u, t = v[0] + v[1], v[0] - v[1], v[2] + v[3], v[2] - v[3]
            out[0 + side], out[4 + side] = p + u, p - u
            out[2 + side], out[6 + side] = q + t, q - t
        return out

    def waves(s, c0, n, row):
        def column(w, carry):
            for h0 in (0, 4):
                blocks = packet(s, w, h0, 4)
                for k in range(4):
                    h = h0 + k
                    line = jnp.concatenate([b[8 * k : 8 * k + 8] for b in blocks], axis=0)
                    wave[w, h + 1, 8 + 64 * s : 72 + 64 * s, :] = line
                    if s == 0:
                        wave[w, h + 1, 264:280, :] = line[:16]
                    if h in (0, 7):
                        edge[s, 0 if h == 0 else 1, w] = line.astype(BF16)
            return carry

        lax.fori_loop(c0, c0 + n, column, 0)

        @pl.when(r > 0)
        def _():
            up(s, c0, n, row).start()

        @pl.when(r < 3)
        def _():
            down(s, c0, n, row).start()

    clip_start = 256 - 64 * z

    def build_taps(s, c0, cn, h_from, h_to):
        r0, n = RANGES[s]
        row = r0 + lax.broadcasted_iota(jnp.int32, (n, C), 0) - clip_start
        outside = [(row >= 0) & (row < 2), row == 0, None]

        def line(h, carry):
            for w in range(c0, c0 + cn):
                for k in range(3):
                    v = wave[w, h, 8 + r0 + k - 2 : 8 + r0 + k - 2 + n, :]
                    if k < 2:
                        v = jnp.where(outside[k], 0.0, v)
                    taps[k, w, h, r0 : r0 + n, :] = v.astype(BF16)
            return carry

        lax.fori_loop(h_from, h_to, line, 0)

    def take_halo(s, c0, n, row):
        @pl.when(r > 0)
        def _():
            down(s, c0, n, row).wait_recv()

        @pl.when(r < 3)
        def _():
            up(s, c0, n, row).wait_recv()

        def column(w, carry):
            for side, h in ((0, 0), (1, 9)):
                line = halo[s, side, w].astype(F32)
                wave[w, h, 8 + 64 * s : 72 + 64 * s, :] = line
                if s == 0:
                    wave[w, h, 264:280, :] = line[:16]
            return carry

        lax.fori_loop(c0, c0 + n, column, 0)

    noted = []

    def merge(a, b):
        (na, ma, qa), (nb, mb, qb) = a, b
        n = na + nb
        delta = mb - ma
        return n, ma + delta * (nb / n), qa + qb + delta * delta * (na * nb / n)

    def conv(s, w0, nw, rows, slot, first=None):
        r0, n = RANGES[s]
        parts = []
        for k in range(3):
            for i in range(3):
                for j in range(3):
                    group = [
                        taps[k, w0 + j : w0 + j + nw, pl.ds(h + i, c), r0 : r0 + n, :].reshape(nw * c * n, C)
                        for h, c in rows
                    ]
                    parts.append(group[0] if len(group) == 1 else jnp.concatenate(group, axis=0))
        out = jnp.dot(jnp.concatenate(parts, axis=1), w_vmem[...], preferred_element_type=F32)
        m = out.shape[0]
        mean = jnp.sum(out, axis=0, keepdims=True) * (1.0 / m)
        d = out - mean
        st[1, pl.ds(slot, 1), :] = mean
        st[2, pl.ds(slot, 1), :] = jnp.sum(d * d, axis=0, keepdims=True)
        if first is not None:
            @pl.when(first)
            def _():
                ref_mean[...] = mean

        kept = (out - ref_mean[...]).astype(BF16)
        pieces, base = [], 0
        for h, c in rows:
            pieces.append(kept[base : base + nw * c * n].reshape(nw, c, n, CO))
            base += nw * c * n
        return pieces

    def conv_pairs(s, hooks):
        r0, n = RANGES[s]

        def chunk(m, carry):
            [piece] = conv(s, 0, 4, [(1 + 2 * m, 2)], m, m == 0 if s == 0 else None)
            for w in range(4):
                for a in range(2):
                    lane = ((1 - a) * 2 + w % 2) * CO
                    acc[m + a, w // 2, r0 : r0 + n, lane : lane + CO] = piece[w, a]
            if hooks is not None:
                hooks(m)
            return carry

        lax.fori_loop(0, 3, chunk, 0)
        noted.extend((8 * n, m) for m in range(3))

    def conv_all(s, w0, nw, rows, slot):
        r0, n = RANGES[s]
        pieces = conv(s, w0, nw, rows, slot)
        for (h, c), piece in zip(rows, pieces):
            for w in range(nw):
                for a in range(c):
                    lane = ((h + a) % 2 * 2 + (w0 + w) % 2) * CO
                    acc[(h + a) // 2, (w0 + w) // 2, r0 : r0 + n, lane : lane + CO] = piece[w, a]
        noted.append((nw * sum(c for _, c in rows) * n, slot))

    EDGES = [(0, 1), (7, 1)]

    def out_copies(s):
        copies = []
        for i, (first, n) in enumerate(PIECES[s]):
            t = (64 * z + first) % 256
            copies.append(
                pltpu.make_async_copy(
                    acc.at[:, :, pl.ds(first, n), :],
                    conv_out.at[:, :, pl.ds(pl.multiple_of(t, 16), n), :],
                    o_s.at[s, i]))
        return copies

    def finish(s):
        total = None if s == 0 else (done[0], st[0, 0:1, :], st[0, 1:2, :])
        for n, slot in noted:
            term = (n, st[1, slot : slot + 1, :], st[2, slot : slot + 1, :])
            total = term if total is None else merge(total, term)
        noted.clear()
        st[0, 0:1, :] = total[1]
        st[0, 1:2, :] = total[2]
        done[0] = total[0]
        for copy in out_copies(s):
            copy.start()

    done = [0]

    def arrive(s):
        if s == 0:
            own.wait()
        for d in range(4):
            across(s, d).wait_recv()

    def hook(*three):
        def run(m):
            for i, (s, d) in enumerate(three):
                @pl.when(m == i)
                def _(s=s, d=d):
                    forward(s, d)

        return run

    def stage(s, hooks):
        arrive(s)
        waves(s, 0, 6, s)
        build_taps(s, 0, 6, 1, 9)
        conv_pairs(s, hooks)
        take_halo(s, 0, 6, s)
        build_taps(s, 0, 6, 0, 1)
        build_taps(s, 0, 6, 9, 10)
        conv_all(s, 0, 4, EDGES, 3)
        finish(s)

    for s, d in ORDER:
        plane(s, d).start()
    own.start()
    across(0, 0, True).start()
    for d in (1, 3, 2):
        forward(0, d)
    forward(1, 0)
    weights.wait()
    stage(0, hook((1, 1), (1, 3), (1, 2)))
    for d in (0, 1, 3):
        forward(3, d)
    stage(1, hook((3, 2), (2, 0), (2, 1)))
    for d in (3, 2):
        forward(2, d)
    stage(3, None)
    stage(2, None)

    mean, sq = st[0, 0:1, :], st[0, 1:2, :]
    held = float(done[0])
    axes = (
        (8, 4 * y + r, line_of, lambda i: 4 * ((y + i // 4) & 1) + ((r + i) & 3)),
        (16, 4 * z + x, plane_of, lambda i: 4 * ((z + i // 4) & 3) + ((x + i) & 3)),
    )
    base, shares = 0, []
    for level, (size, mine, peer, slot) in enumerate(axes):
        sums[base + mine, :, :CO] = mean
        sums[base + mine, :, CO:] = sq
        here = [
            pltpu.make_async_remote_copy(
                src_ref=sums.at[base + mine], dst_ref=sums.at[base + mine],
                send_sem=st_s.at[level, i], recv_sem=st_r.at[level, i],
                device_id=peer(i), device_id_type=MESH)
            for i in range(1, size)
        ]
        for share in here:
            share.start()
        for share in here:
            share.wait_recv()
        shares += here
        means = [sums[base + i, :, :CO] for i in range(size)]
        mean = sum(means) * (1.0 / size)
        sq = sum(sums[base + i, :, CO:] for i in range(size))
        sq = sq + held * sum((m - mean) * (m - mean) for m in means)
        held = held * size
        base += size

    lane = lax.broadcasted_iota(jnp.int32, (1, CO), 1)

    def over_group(v):
        for bit in (1, 2, 4):
            v = v + jnp.where(lane & bit == 0, pltpu.roll(v, CO - bit, 1), pltpu.roll(v, bit, 1))
        return v

    group_mean = over_group(mean) * (1.0 / 8)
    d = mean - group_mean
    variance = over_group(sq + held * d * d) * (1.0 / (8 * held))
    scale = 0.5 * gain[...] / jnp.sqrt(variance + 1e-05)
    shift = (ref_mean[...] - group_mean) * scale + 0.5 * bias[...]
    scale_out[...] = jnp.concatenate([scale] * 4, axis=1)
    shift_out[...] = jnp.concatenate([shift] * 4, axis=1)

    for share in shares:
        share.wait_send()
    for s in range(4):
        for copy in out_copies(s):
            copy.wait()
        for d in range(4):
            across(s, d).wait_send()
            if s or d:
                plane(s, d).wait_send()
        for c0, n, row in ((0, 6, s),):

            @pl.when(r > 0)
            def _():
                up(s, c0, n, row).wait_send()

            @pl.when(r < 3)
            def _():
                down(s, c0, n, row).wait_send()


def per_device(video, conv_weight, norm_gain, norm_bias):
    vmem = pl.BlockSpec(memory_space=pltpu.VMEM)
    anywhere = pl.BlockSpec(memory_space=pl.ANY)
    dma = pltpu.SemaphoreType.DMA
    conv, scale, shift = pl.pallas_call(
        exchange_conv,
        out_shape=(
            jax.ShapeDtypeStruct((4, 2, 256, 1024), BF16),
            jax.ShapeDtypeStruct((1, 1024), F32),
            jax.ShapeDtypeStruct((1, 1024), F32),
        ),
        in_specs=[anywhere, anywhere, vmem, vmem],
        out_specs=(anywhere, vmem, vmem),
        scratch_shapes=[
            pltpu.VMEM((8, 8, 128, C), BF16),
            pltpu.VMEM((130, 64, C), BF16),
            pltpu.VMEM((4, 4, 10, 64, C), BF16),
            pltpu.VMEM((4, 4, 6, 64, C), BF16),
            pltpu.VMEM((4, 2, 6, 64, C), BF16),
            pltpu.VMEM((4, 2, 6, 64, C), BF16),
            pltpu.VMEM((6, 10, 8 + T_ROWS, C), F32),
            pltpu.VMEM((3, 6, 10, T_ROWS, C), BF16),
            pltpu.VMEM((4, 2, T_ROWS, 1024), BF16),
            pltpu.VMEM((27 * C, CO), BF16),
            pltpu.VMEM((3, 8, CO), F32),
            pltpu.VMEM((24, 1, 2 * CO), F32),
            pltpu.VMEM((1, CO), F32),
            dma((4, 4)), dma((4, 4)),
            dma((5, 4)), dma((5, 4)),
            dma,
            dma((5, 2)), dma((5, 2)),
            dma((2, 16)), dma((2, 16)),
            dma, dma, dma((4, 2)),
        ],
        compiler_params=pltpu.CompilerParams(
            collective_id=0, has_side_effects=True, vmem_limit_bytes=60 << 20
        ),
        cost_estimate=pl.CostEstimate(
            flops=2 * 8192 * 3456 * 256, bytes_accessed=16 << 20, transcendentals=0
        ),
    )(video, conv_weight.reshape(27 * C, CO), norm_gain.reshape(1, CO), norm_bias.reshape(1, CO))
    half = conv.astype(F32) * scale[0] + shift[0]
    return (half + half * jnp.tanh(half)).astype(BF16)


def solution(mesh):
    placed = (P("tm", "rows", None, None), P(), P(), P())
    return jax.shard_map(
        per_device,
        mesh=mesh,
        in_specs=placed,
        out_specs=P("rows", "tm", None, None),
        check_vma=False,
    )
```
